32 devices in a mesh: worker: 4 (over z), fsdp: 8 (over y, x, core).
Axes of the slice: x: 2, y: 2, z: 4, core: 2. Of those that a mesh axis runs over, the one named last changes fastest.
Arguments:
- outer_weights: float32 [4, 2, 2048, 512], P('worker', None, 'fsdp'), may hold values from -6 to 6
- pseudo_grad: float32 [4, 2, 2048, 512], P('worker', None, 'fsdp'), may hold values from -6 to 6
- momentum: float32 [4, 2, 2048, 512], P('worker', None, 'fsdp'), may hold values from -6 to 6
- partner: int32 [4], replicated, may hold values from 0 to 3, as said below
Outputs:
- momentum_next: float32 [4, 2, 2048, 512], P('worker', None, 'fsdp')
- weights_full: bfloat16 [4, 2, 2048, 512], P('worker')
The draws below stay inside these ranges and needn't reach their ends.
Inputs may be any that keep to these rules, and one draw needn't show every extreme that they name: partner[partner[w]] = w and partner[w] != w for every replica w.
All inputs are finite; a program needn't handle non-finite values.
Results may differ from the reference program's by a relative error of at most 0.001.
Values may be sent and summed in bfloat16 or wider, within the bound.
A program may use at most 64 MiB of HBM per device.

```python
import jax
import jax.numpy as jnp

D_WIN = 2048
KV = 512
MATS = 2
WORKERS = 4


def draw_partner(key, part):
    key = jax.random.fold_in(key, 7)
    order = jax.random.permutation(key, WORKERS).astype(jnp.int32)
    swapped = order.reshape(-1, 2)[:, ::-1].reshape(-1)
    return jnp.zeros((WORKERS,), jnp.int32).at[order].set(swapped)


def steps_of(stream_key, dims, shards, smallest, top_value):
    factor_of = 1.0
    for axis_at, parts in shards:
        draws = jax.random.uniform(jax.random.fold_in(jax.random.fold_in(stream_key, 6), axis_at), (parts,), jnp.float32, smallest / len(shards), top_value / len(shards))
        factor_of = factor_of * jnp.repeat(jnp.exp(draws), dims[axis_at] // parts).reshape((-1,) + (1,) * (len(dims) - 1 - axis_at))
    return factor_of


def bell_draw(rng, extent, scale, most, cuts=(), held_as=jnp.bfloat16):
    values = jax.random.normal(rng, extent, jnp.float32) * scale
    if len(cuts) > 0:
        values = steps_of(rng, extent, cuts, -0.22, 0.18) * values
    return jnp.clip(values, min=-most, max=most).astype(held_as)


def setup_inputs(seed: int = 0) -> dict:
    streams_of = jax.random.split(jax.random.key(seed), 5)
    return {
        "outer_weights": bell_draw(streams_of[0], (WORKERS, MATS, D_WIN, KV), 1.0, 6.0, ((0, 4), (2, 8)), jnp.float32),
        "pseudo_grad": bell_draw(streams_of[1], (WORKERS, MATS, D_WIN, KV), 1.0, 6.0, ((0, 4), (2, 8)), jnp.float32),
        "momentum": bell_draw(streams_of[2], (WORKERS, MATS, D_WIN, KV), 1.0, 6.0, ((0, 4), (2, 8)), jnp.float32),
        "partner": draw_partner(jax.random.fold_in(streams_of[4], 71), 0),
    }


momentum_decay = 0.9
outer_rate = 0.7
pull_rate = 0.6


def update(weights, delta, moment, mate_weights, mate_delta):
    pair_delta = (delta + mate_delta) * 0.5
    pair_weights = (weights + mate_weights) * 0.5
    moment_next = momentum_decay * moment + pair_delta
    new_weights = weights - outer_rate * (momentum_decay * moment_next + pair_delta) - pull_rate * (weights - pair_weights)
    return new_weights, moment_next


def reference(outer_weights, pseudo_grad, momentum, partner):
    mate_weights = jnp.take(outer_weights, partner, axis=0)
    mate_delta = jnp.take(pseudo_grad, partner, axis=0)
    new_weights, moment_next = update(outer_weights, pseudo_grad, momentum, mate_weights, mate_delta)
    return moment_next, new_weights.astype(jnp.bfloat16)
```

```python
import functools

import jax
import jax.numpy as jnp
from jax import lax
from jax.experimental import pallas as pl
from jax.experimental.pallas import tpu as pltpu
from jax.sharding import PartitionSpec as P

MESH = pl.DeviceIdType.MESH

momentum_decay = 0.9
outer_rate = 0.7
pull_rate = 0.6

LANES = 128
SUB = 8
STEPS = 32767.0
PARTS = 8


def finish(weights, moment, pair_delta, pair_weights):
    moment_next = momentum_decay * moment + pair_delta
    new_weights = (
        weights
        - outer_rate * (momentum_decay * moment_next + pair_delta)
        - pull_rate * (weights - pair_weights)
    )
    return (new_weights, moment_next)


def gathered_body(outer_weights, pseudo_grad, momentum, partner):
    mate_index = partner[lax.axis_index("worker")]
    pieces = (
        lax.all_gather(outer_weights, "worker", axis=0, tiled=True),
        lax.all_gather(pseudo_grad, "worker", axis=0, tiled=True),
    )
    first = lax.dynamic_slice_in_dim(pieces[0], mate_index, 1, 0)
    second = lax.dynamic_slice_in_dim(pieces[1], mate_index, 1, 0)
    pair_delta = (pseudo_grad + second) * 0.5
    pair_weights = (outer_weights + first) * 0.5
    new_weights, moment_next = finish(outer_weights, momentum, pair_delta, pair_weights)
    weights_full = lax.all_gather(new_weights.astype(jnp.bfloat16), "fsdp", axis=2, tiled=True)
    return (moment_next, weights_full)


def mate_of(worker, matching):
    if matching == 1:
        return worker + 1 - 2 * lax.rem(worker, 2)
    if matching == 2:
        return lax.rem(worker + 2, 4)
    return 3 - worker


def pair_kernel(
    matching,
    w_ref, g_ref, m_ref,
    next_ref, full_ref,
    scale_out, scale_in, q_out, q_in, fresh,
    scale_send, scale_recv, q_send, q_recv,
    own_sem, direct_send, direct_recv, core_send, core_recv,
):
    mats, rows, cols = w_ref.shape[1:]
    height = mats * rows // PARTS
    per_mat = rows // height
    groups = height // SUB
    pieces = cols // LANES

    worker, spot = lax.axis_index("worker"), lax.axis_index("fsdp")
    mate = mate_of(worker, matching)
    core = lax.rem(spot, 2)
    chip = lax.div(spot, 2)
    along_x, along_y = lax.rem(chip, 2), lax.div(chip, 2)
    other = 1 - core

    def place(x, y, c):
        return (y * 2 + x) * 2 + c

    chips = (
        (along_x, along_y),
        (1 - along_x, along_y),
        (along_x, 1 - along_y),
        (1 - along_x, 1 - along_y),
    )
    twins = [place(x, y, core) for x, y in chips]
    neighbour = place(along_x, along_y, other)
    peers = [(mate, spot), (worker, neighbour)] + [(worker, t) for t in twins[1:]]

    barrier = pltpu.get_barrier_semaphore()
    for peer in peers:
        pl.semaphore_signal(barrier, inc=1, device_id=peer, device_id_type=MESH)

    for number, ref in enumerate((w_ref, g_ref)):
        def largest(part, top, ref=ref):
            mat, first = lax.div(part, per_mat), lax.rem(part, per_mat) * height
            for piece in range(pieces):
                tile = ref[0, mat, pl.ds(pl.multiple_of(first, height), height), piece * LANES : (piece + 1) * LANES]
                top = jnp.maximum(top, jnp.max(jnp.abs(tile).reshape(groups, SUB, LANES), axis=0))
            return top

        scale_out[number] = lax.fori_loop(0, PARTS, largest, jnp.full((SUB, LANES), 1e-30, jnp.float32))

    pl.semaphore_wait(barrier, len(peers))

    def scales():
        return pltpu.make_async_remote_copy(
            scale_out, scale_in, scale_send, scale_recv, device_id=(mate, spot), device_id_type=MESH
        )

    scales().start()

    def exchange(part):
        return pltpu.make_async_remote_copy(
            q_out.at[part], q_in.at[part], q_send.at[part], q_recv.at[part],
            device_id=(mate, spot), device_id_type=MESH,
        )

    def code(part, _):
        mat, first = lax.div(part, per_mat), lax.rem(part, per_mat) * height
        at = pl.ds(pl.multiple_of(first, height), height)
        for number, ref in enumerate((w_ref, g_ref)):
            inverse = STEPS / scale_out[number]
            for piece in range(pieces):
                lanes = slice(piece * LANES, (piece + 1) * LANES)
                tile = ref[0, mat, at, lanes].reshape(groups, SUB, LANES)
                level = (tile * inverse[None] + 32768.5).astype(jnp.int32) - 32768
                q_out[part, number, :, lanes] = level.reshape(height, LANES).astype(jnp.int16)
        exchange(part).start()
        return 0

    lax.fori_loop(0, PARTS, code, 0)

    scales().wait()

    def rows_of(owner, part):
        mat, first = lax.div(part, per_mat), lax.rem(part, per_mat) * height
        return full_ref.at[0, mat, pl.ds(pl.multiple_of(owner * rows + first, height), height), :]

    def own(part):
        return pltpu.make_async_copy(fresh.at[part], rows_of(spot, part), own_sem.at[part])

    def direct(part, way):
        return pltpu.make_async_remote_copy(
            fresh.at[part], rows_of(spot, part), direct_send.at[way - 1, part], direct_recv.at[way - 1, part],
            device_id=(worker, twins[way]), device_id_type=MESH,
        )

    def across_cores(part, way):
        source = fresh.at[part] if way == 0 else rows_of(twins[way], part)
        return pltpu.make_async_remote_copy(
            source, rows_of(twins[way], part), core_send.at[way, part], core_recv.at[way, part],
            device_id=(worker, neighbour), device_id_type=MESH,
        )

    def update(part, _):
        mat, first = lax.div(part, per_mat), lax.rem(part, per_mat) * height
        at = pl.ds(pl.multiple_of(first, height), height)
        exchange(part).wait_recv()
        back = [scale_in[number] * (1.0 / STEPS) for number in range(2)]
        for piece in range(pieces):
            lanes = slice(piece * LANES, (piece + 1) * LANES)
            got = [
                (
                    q_in[part, number, :, lanes].astype(jnp.int32).astype(jnp.float32).reshape(groups, SUB, LANES)
                    * back[number][None]
                ).reshape(height, LANES)
                for number in range(2)
            ]
            weights, delta, moment = (ref[0, mat, at, lanes] for ref in (w_ref, g_ref, m_ref))
            new, moment_next = finish(weights, moment, (delta + got[1]) * 0.5, (weights + got[0]) * 0.5)
            next_ref[0, mat, at, lanes] = moment_next
            fresh[part, :, lanes] = new.astype(jnp.bfloat16)
        for way in (3, 1, 2):
            direct(part, way).start()
        across_cores(part, 0).start()
        own(part).start()
        return 0

    def pass_on(part, _):
        for way in (1, 2, 3):
            direct(part, way).wait_recv()
            across_cores(part, way).start()
        return 0

    def both(part, _):
        update(part, 0)
        pass_on(part - 1, 0)
        return 0

    update(0, 0)
    lax.fori_loop(1, PARTS, both, 0)
    pass_on(PARTS - 1, 0)

    def drain(part, _):
        exchange(part).wait_send()
        own(part).wait()
        for way in (1, 2, 3):
            direct(part, way).wait_send()
        for way in range(4):
            across_cores(part, way).wait()
        return 0

    lax.fori_loop(0, PARTS, drain, 0)


def paired_call(matching, workers, spots, w, g, m):
    _, mats, rows, cols = w.shape
    height = mats * rows // PARTS
    dma = pltpu.SemaphoreType.DMA
    return pl.pallas_call(
        functools.partial(pair_kernel, matching),
        out_shape=(
            jax.ShapeDtypeStruct(m.shape, jnp.float32),
            jax.ShapeDtypeStruct((1, mats, rows * spots, cols), jnp.bfloat16),
        ),
        in_specs=[pl.BlockSpec(memory_space=pltpu.VMEM)] * 3,
        out_specs=(pl.BlockSpec(memory_space=pltpu.VMEM), pl.BlockSpec(memory_space=pl.ANY)),
        scratch_shapes=[
            pltpu.VMEM((2, SUB, LANES), jnp.float32),
            pltpu.VMEM((2, SUB, LANES), jnp.float32),
            pltpu.VMEM((PARTS, 2, height, cols), jnp.int16),
            pltpu.VMEM((PARTS, 2, height, cols), jnp.int16),
            pltpu.VMEM((PARTS, height, cols), jnp.bfloat16),
            dma, dma, dma((PARTS,)), dma((PARTS,)),
            dma((PARTS,)), dma((3, PARTS)), dma((3, PARTS)), dma((4, PARTS)), dma((4, PARTS)),
        ],
        compiler_params=pltpu.CompilerParams(
            collective_id=matching, has_side_effects=True, vmem_limit_bytes=40 * 1024 * 1024
        ),
        cost_estimate=pl.CostEstimate(flops=12 * w.size, bytes_accessed=20 * w.size, transcendentals=0),
        name="matching_%d" % matching,
    )(w, g, m)


def paired_body(workers, spots, outer_weights, pseudo_grad, momentum, partner):
    calls = [functools.partial(paired_call, matching, workers, spots) for matching in (1, 2, 3)]
    return tuple(lax.switch(partner[0] - 1, calls, outer_weights, pseudo_grad, momentum))


def solution(mesh):
    workers, spots = mesh.shape["worker"], mesh.shape["fsdp"]
    body = gathered_body
    if workers == 4 and spots == 8:
        body = functools.partial(paired_body, workers, spots)
    placed = (
        P("worker", None, "fsdp", None),
        P("worker", None, "fsdp", None),
        P("worker", None, "fsdp", None),
        P(),
    )
    return jax.shard_map(
        body,
        mesh=mesh,
        in_specs=placed,
        out_specs=(P("worker", None, "fsdp", None), P("worker", None, None, None)),
        check_vma=False,
    )
```

```python
import functools

import jax
import jax.numpy as jnp
from jax import lax
from jax.experimental import pallas as pl
from jax.experimental.pallas import tpu as pltpu
from jax.sharding import PartitionSpec as P

MESH = pl.DeviceIdType.MESH

momentum_decay = 0.9
outer_rate = 0.7
pull_rate = 0.6

LANES = 128
SUB = 8
STEPS = 32767.0
PARTS = 8
LAG = 2
SLICES = 4


def finish(weights, moment, pair_delta, pair_weights):
    moment_next = momentum_decay * moment + pair_delta
    new_weights = (
        weights
        - outer_rate * (momentum_decay * moment_next + pair_delta)
        - pull_rate * (weights - pair_weights)
    )
    return (new_weights, moment_next)


def gathered_body(outer_weights, pseudo_grad, momentum, partner):
    mate_index = partner[lax.axis_index("worker")]
    pieces = (
        lax.all_gather(outer_weights, "worker", axis=0, tiled=True),
        lax.all_gather(pseudo_grad, "worker", axis=0, tiled=True),
    )
    first = lax.dynamic_slice_in_dim(pieces[0], mate_index, 1, 0)
    second = lax.dynamic_slice_in_dim(pieces[1], mate_index, 1, 0)
    pair_delta = (pseudo_grad + second) * 0.5
    pair_weights = (outer_weights + first) * 0.5
    new_weights, moment_next = finish(outer_weights, momentum, pair_delta, pair_weights)
    weights_full = lax.all_gather(new_weights.astype(jnp.bfloat16), "fsdp", axis=2, tiled=True)
    return (moment_next, weights_full)


def mate_of(worker, matching):
    if matching == 1:
        return worker + 1 - 2 * lax.rem(worker, 2)
    if matching == 2:
        return lax.rem(worker + 2, 4)
    return 3 - worker


def pair_kernel(
    matching, mats,
    w_hbm, g_hbm, m_hbm,
    next_ref, full_ref,
    w_ref, g_ref, m_ref, scale_out, scale_in, q_out, q_in,
    load_sem, scale_send, scale_recv, q_send, q_recv,
    direct_send, direct_recv, core_send, core_recv,
):
    total, cols = w_ref.shape
    rows = total // mats
    height = total // PARTS
    per_mat = rows // height
    groups = height // SUB
    pieces = cols // LANES
    all_rows = full_ref.shape[0] // mats

    worker, spot = lax.axis_index("worker"), lax.axis_index("fsdp")
    mate = mate_of(worker, matching)
    core = lax.rem(spot, 2)
    chip = lax.div(spot, 2)
    along_x, along_y = lax.rem(chip, 2), lax.div(chip, 2)

    def place(x, y, c):
        return (y * 2 + x) * 2 + c

    chips = (
        (along_x, along_y),
        (1 - along_x, along_y),
        (along_x, 1 - along_y),
        (1 - along_x, 1 - along_y),
    )
    twins = [place(x, y, core) for x, y in chips]
    neighbour = place(along_x, along_y, 1 - core)
    peers = [(mate, spot), (worker, neighbour)] + [(worker, t) for t in twins[1:]]

    def load(source, target, first, count, number):
        return pltpu.make_async_copy(
            source.at[pl.ds(first, count)], target.at[pl.ds(first, count)], load_sem.at[number]
        )

    loads = [
        load(w_hbm, w_ref, 0, height, 0),
        load(g_hbm, g_ref, 0, height, 1),
        load(w_hbm, w_ref, height, total - height, 2),
        load(g_hbm, g_ref, height, total - height, 3),
        load(m_hbm, m_ref, 0, total, 4),
    ]
    for copy in loads:
        copy.start()

    barrier = pltpu.get_barrier_semaphore()
    for peer in peers:
        pl.semaphore_signal(barrier, inc=1, device_id=peer, device_id_type=MESH)

    def at(part):
        return pl.ds(pl.multiple_of(part * height, height), height)

    def to_mate(part):
        return [
            pltpu.make_async_remote_copy(
                out.at[part], into.at[part], sent.at[part], came.at[part],
                device_id=(mate, spot), device_id_type=MESH,
            )
            for out, into, sent, came in (
                (scale_out, scale_in, scale_send, scale_recv),
                (q_out, q_in, q_send, q_recv),
            )
        ]

    def code(part):
        for number, ref in enumerate((w_ref, g_ref)):
            tiles = [
                ref[at(part), piece * LANES : (piece + 1) * LANES].reshape(groups, SUB, LANES)
                for piece in range(pieces)
            ]
            top = jnp.full((SUB, LANES), 1e-30, jnp.float32)
            for tile in tiles:
                top = jnp.maximum(top, jnp.max(jnp.abs(tile), axis=0))
            scale_out[part, number] = top
            inverse = STEPS / top
            for piece, tile in enumerate(tiles):
                level = (tile * inverse[None] + 32768.5).astype(jnp.int32) - 32768
                q_out[part, number, :, piece * LANES : (piece + 1) * LANES] = level.reshape(height, LANES).astype(
                    jnp.int16
                )

    def send(part):
        for copy in to_mate(part):
            copy.start()

    loads[0].wait()
    loads[1].wait()
    code(0)
    pl.semaphore_wait(barrier, len(peers))
    send(0)
    loads[2].wait()
    loads[3].wait()

    def code_and_send(part, _):
        code(part)
        send(part)
        return 0

    lax.fori_loop(1, PARTS, code_and_send, 0)
    loads[4].wait()

    def first_row(owner, part):
        mat, first = lax.div(part, per_mat), lax.rem(part, per_mat) * height
        return pl.multiple_of(mat * all_rows + owner * rows + first, height)

    def rows_of(owner, part):
        return full_ref.at[pl.ds(first_row(owner, part), height)]

    def direct(part, way):
        return pltpu.make_async_remote_copy(
            rows_of(spot, part), rows_of(spot, part), direct_send.at[way - 1, part], direct_recv.at[way - 1, part],
            device_id=(worker, twins[way]), device_id_type=MESH,
        )

    def across_cores(part, way):
        return pltpu.make_async_remote_copy(
            rows_of(twins[way], part), rows_of(twins[way], part), core_send.at[way, part], core_recv.at[way, part],
            device_id=(worker, neighbour), device_id_type=MESH,
        )

    def update(part):
        for copy in to_mate(part):
            copy.wait_recv()
        back = [scale_in[part, number] * (1.0 / STEPS) for number in range(2)]
        mine = pl.ds(first_row(spot, part), height)
        for piece in range(pieces):
            lanes = slice(piece * LANES, (piece + 1) * LANES)
            got = [
                (
                    q_in[part, number, :, lanes].astype(jnp.int32).astype(jnp.float32).reshape(groups, SUB, LANES)
                    * back[number][None]
                ).reshape(height, LANES)
                for number in range(2)
            ]
            weights, delta, moment = (ref[at(part), lanes] for ref in (w_ref, g_ref, m_ref))
            new, moment_next = finish(weights, moment, (delta + got[1]) * 0.5, (weights + got[0]) * 0.5)
            next_ref[at(part), lanes] = moment_next
            full_ref[mine, lanes] = new.astype(jnp.bfloat16)
        for way in (3, 1, 2):
            direct(part, way).start()
        across_cores(part, 0).start()

    def pass_on(part):
        for way in (1, 2, 3):
            direct(part, way).wait_recv()
            across_cores(part, way).start()

    def head(part, _):
        update(part)
        return 0

    def both(part, _):
        update(part)
        pass_on(part - LAG)
        return 0

    def tail(part, _):
        pass_on(part)
        return 0

    lax.fori_loop(0, LAG, head, 0)
    lax.fori_loop(LAG, PARTS, both, 0)
    lax.fori_loop(PARTS - LAG, PARTS, tail, 0)

    def drain(part, _):
        for copy in to_mate(part):
            copy.wait_send()
        for way in (1, 2, 3):
            direct(part, way).wait_send()
        for way in range(4):
            across_cores(part, way).wait()
        return 0

    lax.fori_loop(0, PARTS, drain, 0)


def paired_call(matching, spots, w, g, m):
    _, mats, rows, cols = w.shape
    total = mats * rows
    height = total // PARTS
    dma = pltpu.SemaphoreType.DMA
    vmem = pltpu.VMEM
    return pl.pallas_call(
        functools.partial(pair_kernel, matching, mats),
        out_shape=(
            jax.ShapeDtypeStruct((total, cols), jnp.float32),
            jax.ShapeDtypeStruct((total * spots, cols), jnp.bfloat16),
        ),
        in_specs=[pl.BlockSpec(memory_space=pl.ANY)] * 3,
        out_specs=(pl.BlockSpec(memory_space=vmem), pl.BlockSpec(memory_space=vmem)),
        scratch_shapes=[
            vmem((total, cols), jnp.float32),
            vmem((total, cols), jnp.float32),
            vmem((total, cols), jnp.float32),
            vmem((PARTS, 2, SUB, LANES), jnp.float32),
            vmem((PARTS, 2, SUB, LANES), jnp.float32),
            vmem((PARTS, 2, height, cols), jnp.int16),
            vmem((PARTS, 2, height, cols), jnp.int16),
            dma((5,)), dma((PARTS,)), dma((PARTS,)), dma((PARTS,)), dma((PARTS,)),
            dma((3, PARTS)), dma((3, PARTS)), dma((4, PARTS)), dma((4, PARTS)),
        ],
        compiler_params=pltpu.CompilerParams(
            collective_id=matching, has_side_effects=True, vmem_limit_bytes=40 * 1024 * 1024
        ),
        cost_estimate=pl.CostEstimate(flops=12 * w.size, bytes_accessed=20 * w.size, transcendentals=0),
        name="matching_%d" % matching,
    )(*(a.reshape(total, cols) for a in (w, g, m)))


def publish_kernel(next_ref, full_ref, next_hbm, full_hbm, sem):
    step = full_ref.shape[0] // SLICES
    copies = [
        pltpu.make_async_copy(
            full_ref.at[pl.ds(part * step, step)], full_hbm.at[pl.ds(part * step, step)], sem.at[part]
        )
        for part in range(SLICES)
    ]
    copies.append(pltpu.make_async_copy(next_ref, next_hbm, sem.at[SLICES]))
    for copy in copies:
        copy.start()
    for copy in copies:
        copy.wait()


def publish(moment_next, full):
    return pl.pallas_call(
        publish_kernel,
        out_shape=[jax.ShapeDtypeStruct(a.shape, a.dtype) for a in (moment_next, full)],
        in_specs=[pl.BlockSpec(memory_space=pltpu.VMEM)] * 2,
        out_specs=[pl.BlockSpec(memory_space=pl.ANY)] * 2,
        scratch_shapes=[pltpu.SemaphoreType.DMA((SLICES + 1,))],
        name="publish",
    )(moment_next, full)


def paired_body(spots, outer_weights, pseudo_grad, momentum, partner):
    calls = [functools.partial(paired_call, matching, spots) for matching in (1, 2, 3)]
    moment_next, full = publish(*lax.switch(partner[0] - 1, calls, outer_weights, pseudo_grad, momentum))
    _, mats, rows, cols = momentum.shape
    return moment_next.reshape(momentum.shape), full.reshape(1, mats, rows * spots, cols)


def solution(mesh):
    workers, spots = mesh.shape["worker"], mesh.shape["fsdp"]
    body = gathered_body
    if workers == 4 and spots == 8:
        body = functools.partial(paired_body, spots)
    placed = (
        P("worker", None, "fsdp", None),
        P("worker", None, "fsdp", None),
        P("worker", None, "fsdp", None),
        P(),
    )
    return jax.shard_map(
        body,
        mesh=mesh,
        in_specs=placed,
        out_specs=(P("worker", None, "fsdp", None), P("worker", None, None, None)),
        check_vma=False,
    )
```

```python
import functools

import jax
import jax.numpy as jnp
from jax import lax
from jax.experimental import pallas as pl
from jax.experimental.pallas import tpu as pltpu
from jax.sharding import PartitionSpec as P

MESH = pl.DeviceIdType.MESH

momentum_decay = 0.9
outer_rate = 0.7
pull_rate = 0.6

LANES = 128
SUB = 8
STEPS = 32767.0
PARTS = 16
LAG = 3
WAIT = 2
SLICES = 4


def finish(weights, moment, pair_delta, pair_weights):
    moment_next = momentum_decay * moment + pair_delta
    new_weights = (
        weights
        - outer_rate * (momentum_decay * moment_next + pair_delta)
        - pull_rate * (weights - pair_weights)
    )
    return (new_weights, moment_next)


def gathered_body(outer_weights, pseudo_grad, momentum, partner):
    mate_index = partner[lax.axis_index("worker")]
    pieces = (
        lax.all_gather(outer_weights, "worker", axis=0, tiled=True),
        lax.all_gather(pseudo_grad, "worker", axis=0, tiled=True),
    )
    first = lax.dynamic_slice_in_dim(pieces[0], mate_index, 1, 0)
    second = lax.dynamic_slice_in_dim(pieces[1], mate_index, 1, 0)
    pair_delta = (pseudo_grad + second) * 0.5
    pair_weights = (outer_weights + first) * 0.5
    new_weights, moment_next = finish(outer_weights, momentum, pair_delta, pair_weights)
    weights_full = lax.all_gather(new_weights.astype(jnp.bfloat16), "fsdp", axis=2, tiled=True)
    return (moment_next, weights_full)


def mate_of(worker, matching):
    if matching == 1:
        return worker + 1 - 2 * lax.rem(worker, 2)
    if matching == 2:
        return lax.rem(worker + 2, 4)
    return 3 - worker


def pair_kernel(
    matching, mats,
    w_hbm, g_hbm, m_hbm,
    next_ref, full_ref,
    w_ref, g_ref, m_ref, scale_out, scale_in, q_out, q_in,
    load_sem, scale_send, scale_recv, q_send, q_recv,
    direct_send, direct_recv, core_send, core_recv,
):
    total, cols = w_ref.shape
    rows = total // mats
    height = total // PARTS
    per_mat = rows // height
    groups = height // SUB
    pieces = cols // LANES
    all_rows = full_ref.shape[0] // mats

    worker, spot = lax.axis_index("worker"), lax.axis_index("fsdp")
    mate = mate_of(worker, matching)
    core = lax.rem(spot, 2)
    chip = lax.div(spot, 2)
    along_x, along_y = lax.rem(chip, 2), lax.div(chip, 2)

    def place(x, y, c):
        return (y * 2 + x) * 2 + c

    chips = (
        (along_x, along_y),
        (1 - along_x, along_y),
        (along_x, 1 - along_y),
        (1 - along_x, 1 - along_y),
    )
    twins = [place(x, y, core) for x, y in chips]
    neighbour = place(along_x, along_y, 1 - core)
    peers = [(mate, spot), (worker, neighbour)] + [(worker, t) for t in twins[1:]]

    barrier = pltpu.get_barrier_semaphore()
    for peer in peers:
        pl.semaphore_signal(barrier, inc=1, device_id=peer, device_id_type=MESH)

    def load(source, target, first, count, number):
        return pltpu.make_async_copy(
            source.at[pl.ds(first, count)], target.at[pl.ds(first, count)], load_sem.at[number]
        )

    loads = [
        load(w_hbm, w_ref, 0, height, 0),
        load(g_hbm, g_ref, 0, height, 1),
        load(w_hbm, w_ref, height, total - height, 2),
        load(g_hbm, g_ref, height, total - height, 3),
        load(m_hbm, m_ref, 0, total, 4),
    ]
    for copy in loads:
        copy.start()

    def at(part):
        return pl.ds(pl.multiple_of(part * height, height), height)

    def to_mate(part):
        return [
            pltpu.make_async_remote_copy(
                out.at[part], into.at[part], sent.at[part], came.at[part],
                device_id=(mate, spot), device_id_type=MESH,
            )
            for out, into, sent, came in (
                (scale_out, scale_in, scale_send, scale_recv),
                (q_out, q_in, q_send, q_recv),
            )
        ]

    def code(part):
        for number, ref in enumerate((w_ref, g_ref)):
            tiles = [
                ref[at(part), piece * LANES : (piece + 1) * LANES].reshape(groups, SUB, LANES)
                for piece in range(pieces)
            ]
            top = jnp.full((SUB, LANES), 1e-30, jnp.float32)
            for tile in tiles:
                top = jnp.maximum(top, jnp.max(jnp.abs(tile), axis=0))
            top = jnp.max(top, axis=0, keepdims=True)
            scale_out[part, number : number + 1, :] = top
            inverse = STEPS / top
            for piece, tile in enumerate(tiles):
                level = (tile * inverse[None] + 32768.5).astype(jnp.int32) - 32768
                q_out[part, number, :, piece * LANES : (piece + 1) * LANES] = level.reshape(height, LANES).astype(
                    jnp.int16
                )

    def send(part):
        for copy in to_mate(part):
            copy.start()

    loads[0].wait()
    loads[1].wait()
    code(0)
    pl.semaphore_wait(barrier, len(peers))
    send(0)
    loads[2].wait()
    loads[3].wait()

    def code_and_send(part, _):
        code(part)
        send(part)
        return 0

    lax.fori_loop(1, PARTS, code_and_send, 0)
    loads[4].wait()

    def first_row(owner, part):
        mat, first = lax.div(part, per_mat), lax.rem(part, per_mat) * height
        return pl.multiple_of(mat * all_rows + owner * rows + first, height)

    def rows_of(owner, part):
        return full_ref.at[pl.ds(first_row(owner, part), height)]

    def direct(part, way):
        return pltpu.make_async_remote_copy(
            rows_of(spot, part), rows_of(spot, part), direct_send.at[way - 1, part], direct_recv.at[way - 1, part],
            device_id=(worker, twins[way]), device_id_type=MESH,
        )

    def across_cores(part, way):
        return pltpu.make_async_remote_copy(
            rows_of(twins[way], part), rows_of(twins[way], part), core_send.at[way, part], core_recv.at[way, part],
            device_id=(worker, neighbour), device_id_type=MESH,
        )

    def update(part):
        for copy in to_mate(part):
            copy.wait_recv()
        back = [scale_in[part, number : number + 1, :] * (1.0 / STEPS) for number in range(2)]
        mine = pl.ds(first_row(spot, part), height)
        for piece in range(pieces):
            lanes = slice(piece * LANES, (piece + 1) * LANES)
            got = [
                (
                    q_in[part, number, :, lanes].astype(jnp.int32).astype(jnp.float32).reshape(groups, SUB, LANES)
                    * back[number][None]
                ).reshape(height, LANES)
                for number in range(2)
            ]
            weights, delta, moment = (ref[at(part), lanes] for ref in (w_ref, g_ref, m_ref))
            new, moment_next = finish(weights, moment, (delta + got[1]) * 0.5, (weights + got[0]) * 0.5)
            next_ref[at(part), lanes] = moment_next
            full_ref[mine, lanes] = new.astype(jnp.bfloat16)
        for way in (3, 1, 2):
            direct(part, way).start()
        across_cores(part, 0).start()

    def pass_on(part):
        for way in (1, 2, 3):
            direct(part, way).wait_recv()
            across_cores(part, way).start()

    def drain(part):
        for copy in to_mate(part):
            copy.wait_send()
        for way in (1, 2, 3):
            direct(part, way).wait_send()
        for way in range(4):
            across_cores(part, way).wait()

    def step(part, _):
        @pl.when(part < PARTS)
        def _():
            update(part)

        @pl.when(jnp.logical_and(part >= LAG, part < PARTS + LAG))
        def _():
            pass_on(part - LAG)

        @pl.when(part >= LAG + WAIT)
        def _():
            drain(part - LAG - WAIT)

        return 0

    lax.fori_loop(0, PARTS + LAG + WAIT, step, 0)


def paired_call(matching, spots, w, g, m):
    _, mats, rows, cols = w.shape
    total = mats * rows
    height = total // PARTS
    dma = pltpu.SemaphoreType.DMA
    vmem = pltpu.VMEM
    return pl.pallas_call(
        functools.partial(pair_kernel, matching, mats),
        out_shape=(
            jax.ShapeDtypeStruct((total, cols), jnp.float32),
            jax.ShapeDtypeStruct((total * spots, cols), jnp.bfloat16),
        ),
        in_specs=[pl.BlockSpec(memory_space=pl.ANY)] * 3,
        out_specs=(pl.BlockSpec(memory_space=vmem), pl.BlockSpec(memory_space=vmem)),
        scratch_shapes=[
            vmem((total, cols), jnp.float32),
            vmem((total, cols), jnp.float32),
            vmem((total, cols), jnp.float32),
            vmem((PARTS, 2, LANES), jnp.float32),
            vmem((PARTS, 2, LANES), jnp.float32),
            vmem((PARTS, 2, height, cols), jnp.int16),
            vmem((PARTS, 2, height, cols), jnp.int16),
            dma((5,)), dma((PARTS,)), dma((PARTS,)), dma((PARTS,)), dma((PARTS,)),
            dma((3, PARTS)), dma((3, PARTS)), dma((4, PARTS)), dma((4, PARTS)),
        ],
        compiler_params=pltpu.CompilerParams(
            collective_id=matching, has_side_effects=True, vmem_limit_bytes=40 * 1024 * 1024
        ),
        cost_estimate=pl.CostEstimate(flops=12 * w.size, bytes_accessed=20 * w.size, transcendentals=0),
        name="matching_%d" % matching,
    )(*(a.reshape(total, cols) for a in (w, g, m)))


def publish_kernel(next_ref, full_ref, next_hbm, full_hbm, sem):
    step = full_ref.shape[0] // SLICES
    copies = [
        pltpu.make_async_copy(
            full_ref.at[pl.ds(part * step, step)], full_hbm.at[pl.ds(part * step, step)], sem.at[part]
        )
        for part in range(SLICES)
    ]
    copies.append(pltpu.make_async_copy(next_ref, next_hbm, sem.at[SLICES]))
    for copy in copies:
        copy.start()
    for copy in copies:
        copy.wait()


def publish(moment_next, full):
    return pl.pallas_call(
        publish_kernel,
        out_shape=[jax.ShapeDtypeStruct(a.shape, a.dtype) for a in (moment_next, full)],
        in_specs=[pl.BlockSpec(memory_space=pltpu.VMEM)] * 2,
        out_specs=[pl.BlockSpec(memory_space=pl.ANY)] * 2,
        scratch_shapes=[pltpu.SemaphoreType.DMA((SLICES + 1,))],
        name="publish",
    )(moment_next, full)


def paired_body(spots, outer_weights, pseudo_grad, momentum, partner):
    calls = [functools.partial(paired_call, matching, spots) for matching in (1, 2, 3)]
    moment_next, full = publish(*lax.switch(partner[0] - 1, calls, outer_weights, pseudo_grad, momentum))
    _, mats, rows, cols = momentum.shape
    return moment_next.reshape(momentum.shape), full.reshape(1, mats, rows * spots, cols)


def solution(mesh):
    workers, spots = mesh.shape["worker"], mesh.shape["fsdp"]
    body = gathered_body
    if workers == 4 and spots == 8:
        body = functools.partial(paired_body, spots)
    placed = (
        P("worker", None, "fsdp", None),
        P("worker", None, "fsdp", None),
        P("worker", None, "fsdp", None),
        P(),
    )
    return jax.shard_map(
        body,
        mesh=mesh,
        in_specs=placed,
        out_specs=(P("worker", None, "fsdp", None), P("worker", None, None, None)),
        check_vma=False,
    )
```

```python
import functools

import jax
import jax.numpy as jnp
from jax import lax
from jax.experimental import pallas as pl
from jax.experimental.pallas import tpu as pltpu
from jax.sharding import PartitionSpec as P

MESH = pl.DeviceIdType.MESH

momentum_decay = 0.9
outer_rate = 0.7
pull_rate = 0.6

LANES = 128
SUB = 8
STEPS = 32767.0
PARTS = 16
LAG = 3
WAIT = 2
SLICES = 4


def finish(weights, moment, pair_delta, pair_weights):
    moment_next = momentum_decay * moment + pair_delta
    new_weights = (
        weights
        - outer_rate * (momentum_decay * moment_next + pair_delta)
        - pull_rate * (weights - pair_weights)
    )
    return (new_weights, moment_next)


def gathered_body(outer_weights, pseudo_grad, momentum, partner):
    mate_index = partner[lax.axis_index("worker")]
    pieces = (
        lax.all_gather(outer_weights, "worker", axis=0, tiled=True),
        lax.all_gather(pseudo_grad, "worker", axis=0, tiled=True),
    )
    first = lax.dynamic_slice_in_dim(pieces[0], mate_index, 1, 0)
    second = lax.dynamic_slice_in_dim(pieces[1], mate_index, 1, 0)
    pair_delta = (pseudo_grad + second) * 0.5
    pair_weights = (outer_weights + first) * 0.5
    new_weights, moment_next = finish(outer_weights, momentum, pair_delta, pair_weights)
    weights_full = lax.all_gather(new_weights.astype(jnp.bfloat16), "fsdp", axis=2, tiled=True)
    return (moment_next, weights_full)


def mate_of(worker, matching):
    if matching == 1:
        return worker + 1 - 2 * lax.rem(worker, 2)
    if matching == 2:
        return lax.rem(worker + 2, 4)
    return 3 - worker


def pair_kernel(
    matching, mats,
    w_hbm, g_hbm, m_hbm,
    next_ref, full_ref,
    w_ref, g_ref, m_ref, scale_out, scale_in, q_out, q_in,
    load_sem, scale_send, scale_recv, q_send, q_recv,
    direct_send, direct_recv, core_send, core_recv,
):
    total, cols = w_ref.shape
    rows = total // mats
    height = total // PARTS
    per_mat = rows // height
    pieces = cols // LANES
    all_rows = full_ref.shape[0] // mats

    worker, spot = lax.axis_index("worker"), lax.axis_index("fsdp")
    mate = mate_of(worker, matching)
    core = lax.rem(spot, 2)
    chip = lax.div(spot, 2)
    along_x, along_y = lax.rem(chip, 2), lax.div(chip, 2)

    def place(x, y, c):
        return (y * 2 + x) * 2 + c

    chips = (
        (along_x, along_y),
        (1 - along_x, along_y),
        (along_x, 1 - along_y),
        (1 - along_x, 1 - along_y),
    )
    twins = [place(x, y, core) for x, y in chips]
    neighbour = place(along_x, along_y, 1 - core)
    peers = [(mate, spot), (worker, neighbour)] + [(worker, t) for t in twins[1:]]

    barrier = pltpu.get_barrier_semaphore()
    for peer in peers:
        pl.semaphore_signal(barrier, inc=1, device_id=peer, device_id_type=MESH)

    def load(source, target, first, count, number):
        return pltpu.make_async_copy(
            source.at[pl.ds(first, count)], target.at[pl.ds(first, count)], load_sem.at[number]
        )

    loads = [
        load(w_hbm, w_ref, 0, rows, 0),
        load(g_hbm, g_ref, 0, rows, 1),
        load(w_hbm, w_ref, rows, total - rows, 2),
        load(g_hbm, g_ref, rows, total - rows, 3),
        load(m_hbm, m_ref, 0, total, 4),
    ]
    for copy in loads:
        copy.start()

    def at(part):
        return pl.ds(pl.multiple_of(part * height, height), height)

    def to_mate(out, into, sent, came, slot):
        return pltpu.make_async_remote_copy(
            out.at[slot], into.at[slot], sent.at[slot], came.at[slot],
            device_id=(mate, spot), device_id_type=MESH,
        )

    levels = functools.partial(to_mate, q_out, q_in, q_send, q_recv)
    scales = functools.partial(to_mate, scale_out, scale_in, scale_send, scale_recv)

    def measure(mat):
        for number, ref in enumerate((w_ref, g_ref)):
            top = jnp.full((SUB, LANES), 1e-30, jnp.float32)
            for piece in range(pieces):
                tile = ref[pl.ds(mat * rows, rows), piece * LANES : (piece + 1) * LANES]
                top = jnp.maximum(top, jnp.max(jnp.abs(tile).reshape(rows // SUB, SUB, LANES), axis=0))
            scale_out[mat, number : number + 1, :] = jnp.max(top, axis=0, keepdims=True)

    def code(part):
        for number, ref in enumerate((w_ref, g_ref)):
            inverse = STEPS / scale_out[lax.div(part, per_mat), number : number + 1, :]
            for piece in range(pieces):
                lanes = slice(piece * LANES, (piece + 1) * LANES)
                level = (ref[at(part), lanes] * inverse + 32768.5).astype(jnp.int32) - 32768
                q_out[part, number, :, lanes] = level.astype(jnp.int16)

    def code_and_send(part, _):
        code(part)
        levels(part).start()
        return 0

    for mat in range(mats):
        if mat < 2:
            loads[2 * mat].wait()
            loads[2 * mat + 1].wait()
        measure(mat)
        if mat == 0:
            code(0)
            pl.semaphore_wait(barrier, len(peers))
        scales(mat).start()
        if mat == 0:
            levels(0).start()
        lax.fori_loop(max(1, mat * per_mat), (mat + 1) * per_mat, code_and_send, 0)
    loads[4].wait()

    def first_row(owner, part):
        mat, first = lax.div(part, per_mat), lax.rem(part, per_mat) * height
        return pl.multiple_of(mat * all_rows + owner * rows + first, height)

    def rows_of(owner, part):
        return full_ref.at[pl.ds(first_row(owner, part), height)]

    def direct(part, way):
        return pltpu.make_async_remote_copy(
            rows_of(spot, part), rows_of(spot, part), direct_send.at[way - 1, part], direct_recv.at[way - 1, part],
            device_id=(worker, twins[way]), device_id_type=MESH,
        )

    def across_cores(part, way):
        return pltpu.make_async_remote_copy(
            rows_of(twins[way], part), rows_of(twins[way], part), core_send.at[way, part], core_recv.at[way, part],
            device_id=(worker, neighbour), device_id_type=MESH,
        )

    def update(part):
        mat = lax.div(part, per_mat)

        @pl.when(lax.rem(part, per_mat) == 0)
        def _():
            scales(mat).wait_recv()

        levels(part).wait_recv()
        back = [scale_in[mat, number : number + 1, :] * (1.0 / STEPS) for number in range(2)]
        mine = pl.ds(first_row(spot, part), height)
        for piece in range(pieces):
            lanes = slice(piece * LANES, (piece + 1) * LANES)
            got = [
                q_in[part, number, :, lanes].astype(jnp.int32).astype(jnp.float32) * back[number]
                for number in range(2)
            ]
            weights, delta, moment = (ref[at(part), lanes] for ref in (w_ref, g_ref, m_ref))
            new, moment_next = finish(weights, moment, (delta + got[1]) * 0.5, (weights + got[0]) * 0.5)
            next_ref[at(part), lanes] = moment_next
            full_ref[mine, lanes] = new.astype(jnp.bfloat16)
        for way in (3, 1, 2):
            direct(part, way).start()
        across_cores(part, 0).start()

    def pass_on(part):
        for way in (1, 2, 3):
            direct(part, way).wait_recv()
            across_cores(part, way).start()

    def drain(part):
        @pl.when(lax.rem(part, per_mat) == 0)
        def _():
            scales(lax.div(part, per_mat)).wait_send()

        levels(part).wait_send()
        for way in (1, 2, 3):
            direct(part, way).wait_send()
        for way in range(4):
            across_cores(part, way).wait()

    def step(part, _):
        @pl.when(part < PARTS)
        def _():
            update(part)

        @pl.when(jnp.logical_and(part >= LAG, part < PARTS + LAG))
        def _():
            pass_on(part - LAG)

        @pl.when(part >= LAG + WAIT)
        def _():
            drain(part - LAG - WAIT)

        return 0

    lax.fori_loop(0, PARTS + LAG + WAIT, step, 0)


def paired_call(matching, spots, w, g, m):
    _, mats, rows, cols = w.shape
    total = mats * rows
    height = total // PARTS
    dma = pltpu.SemaphoreType.DMA
    vmem = pltpu.VMEM
    return pl.pallas_call(
        functools.partial(pair_kernel, matching, mats),
        out_shape=(
            jax.ShapeDtypeStruct((total, cols), jnp.float32),
            jax.ShapeDtypeStruct((total * spots, cols), jnp.bfloat16),
        ),
        in_specs=[pl.BlockSpec(memory_space=pl.ANY)] * 3,
        out_specs=(pl.BlockSpec(memory_space=vmem), pl.BlockSpec(memory_space=vmem)),
        scratch_shapes=[
            vmem((total, cols), jnp.float32),
            vmem((total, cols), jnp.float32),
            vmem((total, cols), jnp.float32),
            vmem((mats, 2, LANES), jnp.float32),
            vmem((mats, 2, LANES), jnp.float32),
            vmem((PARTS, 2, height, cols), jnp.int16),
            vmem((PARTS, 2, height, cols), jnp.int16),
            dma((5,)), dma((mats,)), dma((mats,)), dma((PARTS,)), dma((PARTS,)),
            dma((3, PARTS)), dma((3, PARTS)), dma((4, PARTS)), dma((4, PARTS)),
        ],
        compiler_params=pltpu.CompilerParams(
            collective_id=matching, has_side_effects=True, vmem_limit_bytes=40 * 1024 * 1024
        ),
        cost_estimate=pl.CostEstimate(flops=12 * w.size, bytes_accessed=20 * w.size, transcendentals=0),
        name="matching_%d" % matching,
    )(*(a.reshape(total, cols) for a in (w, g, m)))


def publish_kernel(next_ref, full_ref, next_hbm, full_hbm, sem):
    step = full_ref.shape[0] // SLICES
    copies = [
        pltpu.make_async_copy(
            full_ref.at[pl.ds(part * step, step)], full_hbm.at[pl.ds(part * step, step)], sem.at[part]
        )
        for part in range(SLICES)
    ]
    copies.append(pltpu.make_async_copy(next_ref, next_hbm, sem.at[SLICES]))
    for copy in copies:
        copy.start()
    for copy in copies:
        copy.wait()


def publish(moment_next, full):
    return pl.pallas_call(
        publish_kernel,
        out_shape=[jax.ShapeDtypeStruct(a.shape, a.dtype) for a in (moment_next, full)],
        in_specs=[pl.BlockSpec(memory_space=pltpu.VMEM)] * 2,
        out_specs=[pl.BlockSpec(memory_space=pl.ANY)] * 2,
        scratch_shapes=[pltpu.SemaphoreType.DMA((SLICES + 1,))],
        name="publish",
    )(moment_next, full)


def paired_body(spots, outer_weights, pseudo_grad, momentum, partner):
    calls = [functools.partial(paired_call, matching, spots) for matching in (1, 2, 3)]
    moment_next, full = publish(*lax.switch(partner[0] - 1, calls, outer_weights, pseudo_grad, momentum))
    _, mats, rows, cols = momentum.shape
    return moment_next.reshape(momentum.shape), full.reshape(1, mats, rows * spots, cols)


def solution(mesh):
    workers, spots = mesh.shape["worker"], mesh.shape["fsdp"]
    body = gathered_body
    if workers == 4 and spots == 8:
        body = functools.partial(paired_body, spots)
    placed = (
        P("worker", None, "fsdp", None),
        P("worker", None, "fsdp", None),
        P("worker", None, "fsdp", None),
        P(),
    )
    return jax.shard_map(
        body,
        mesh=mesh,
        in_specs=placed,
        out_specs=(P("worker", None, "fsdp", None), P("worker", None, None, None)),
        check_vma=False,
    )
```
